32 devices in a mesh: dp: 2 (over x), row: 4 (over z), col: 4 (over y, core).
Axes of the slice: x: 2, y: 2, z: 4, core: 2. Of those that a mesh axis runs over, the one named last changes fastest.
Arguments:
- x_in: bfloat16 [16384, 1024], P(('dp', 'col'), 'row'), may hold values from -6 to 6
- ln1_gain: float32 [1024], P('row'), may hold values from 0.5 to 1.5
- ln1_bias: float32 [1024], P('row'), may hold values from -1.5 to 1.5
- w_qkv: bfloat16 [1024, 3072], P('row', 'col'), may hold values from -0.1875 to 0.1875
- bias_qv: float32 [2048], P('col'), may hold values from -1.5 to 1.5
- w_out: bfloat16 [1024, 1024], P('col', 'row'), may hold values from -0.375 to 0.375
- b_out: float32 [1024], P('row'), may hold values from -1.5 to 1.5
- ln2_gain: float32 [1024], P('row'), may hold values from 0.5 to 1.5
- ln2_bias: float32 [1024], P('row'), may hold values from -1.5 to 1.5
- w_up: bfloat16 [1024, 4096], P('row', 'col'), may hold values from -0.1875 to 0.1875
- b_up: float32 [4096], P('col'), may hold values from -1.5 to 1.5
- w_down: bfloat16 [4096, 1024], P('col', 'row'), may hold values from -0.09375 to 0.09375
- b_down: float32 [1024], P('row'), may hold values from -1.5 to 1.5
- grad_out: bfloat16 [16384, 1024], P(('dp', 'col'), 'row'), may hold values from -6 to 6
Outputs:
- out: bfloat16 [16384, 1024], P(('dp', 'col'), 'row')
- grad_input: bfloat16 [16384, 1024], P(('dp', 'col'), 'row')
- grad_ln1_gain: float32 [1024], P('row')
- grad_ln1_bias: float32 [1024], P('row')
- grad_qkv: float32 [1024, 3072], P('row', 'col')
- grad_bias_qv: float32 [2048], P('col')
- grad_w_out: float32 [1024, 1024], P('col', 'row')
- grad_b_out: float32 [1024], P('row')
- grad_ln2_gain: float32 [1024], P('row')
- grad_ln2_bias: float32 [1024], P('row')
- grad_up: float32 [1024, 4096], P('row', 'col')
- grad_b_up: float32 [4096], P('col')
- grad_down: float32 [4096, 1024], P('col', 'row')
- grad_b_down: float32 [1024], P('row')
The draws below stay inside these ranges and needn't reach their ends.
All inputs are finite; a program needn't handle non-finite values.
Results may differ from the reference program's by a relative error of at most 0.0098.
Values may be sent and summed in bfloat16 or wider, within the bound.
A program may use at most 192 MiB of HBM per device.

```python
import jax
import jax.numpy as jnp
from jax import lax

D = 1024
HEADS = 16
HEAD = 64
FF = 4096
LEN = 1024
TOKENS = 16384


def block_scale(stream_key, extent, shards, least, high):
    factor_of, own = 1.0, jax.random.fold_in(stream_key, 6)
    for axis_at, shards_of in shards:
        steps = jnp.exp(jax.random.uniform(jax.random.fold_in(own, axis_at), (shards_of,), jnp.float32, least / len(shards), high / len(shards)))
        factor_of = factor_of * jnp.repeat(steps, extent[axis_at] // shards_of).reshape([-1 if axis == axis_at else 1 for axis in range(len(extent))])
    return factor_of


def noise(stream_key, dims, scale, bound, cuts=(), dtype=jnp.bfloat16):
    factor_of = block_scale(stream_key, dims, cuts, -0.22, 0.18) if cuts else 1.0
    array = jax.random.normal(stream_key, dims, jnp.float32) * scale * factor_of
    return jnp.minimum(jnp.maximum(array, -bound), bound).astype(dtype)


def setup_inputs(seed: int = 0) -> dict:
    key_of = jax.random.split(jax.random.key(seed), 15)
    x_in = noise(key_of[0], (TOKENS, D), 1.0, 6.0, ((0, 8), (1, 4)))
    ln1_gain = jnp.clip(1.0 + 0.1 * jax.random.normal(key_of[1], (D,), jnp.float32), 0.5, 1.5)
    ln1_bias = noise(key_of[2], (D,), 0.3, 1.5, ((0, 4),), jnp.float32)
    w_qkv = noise(key_of[3], (D, 3 * D), D ** -0.5, 0.1875, ((0, 4), (1, 4)))
    bias_qv = noise(key_of[4], (2 * D,), 0.3, 1.5, ((0, 4),), jnp.float32)
    w_out = noise(key_of[5], (D, D), (D // 4) ** -0.5, 0.375, ((0, 4), (1, 4)))
    b_out = noise(key_of[6], (D,), 0.3, 1.5, ((0, 4),), jnp.float32)
    ln2_gain = jnp.clip(1.0 + 0.1 * jax.random.normal(key_of[7], (D,), jnp.float32), 0.5, 1.5)
    ln2_bias = noise(key_of[8], (D,), 0.3, 1.5, ((0, 4),), jnp.float32)
    w_up = noise(key_of[9], (D, FF), D ** -0.5, 0.1875, ((0, 4), (1, 4)))
    b_up = noise(key_of[10], (FF,), 0.3, 1.5, ((0, 4),), jnp.float32)
    w_down = noise(key_of[11], (FF, D), FF ** -0.5, 0.09375, ((0, 4), (1, 4)))
    b_down = noise(key_of[12], (D,), 0.3, 1.5, ((0, 4),), jnp.float32)
    grad_out = noise(key_of[13], (TOKENS, D), 1.0, 6.0, ((0, 8), (1, 4)))
    return {"x_in": x_in, "ln1_gain": ln1_gain, "ln1_bias": ln1_bias, "w_qkv": w_qkv, "bias_qv": bias_qv, "w_out": w_out, "b_out": b_out, "ln2_gain": ln2_gain, "ln2_bias": ln2_bias, "w_up": w_up, "b_up": b_up, "w_down": w_down, "b_down": b_down, "grad_out": grad_out}


@jax.custom_vjp
def low(v):
    return lax.optimization_barrier(v.astype(jnp.bfloat16)).astype(jnp.float32)

@jax.custom_vjp
def low_back(v):
    return v

def low_keep(v):
    return (low(v), None)

def low_pass(kept, grad):
    return (grad,)

def back_keep(v):
    return (v, None)

def back_low(kept, grad):
    return (low(grad),)
low.defvjp(low_keep, low_pass)
low_back.defvjp(back_keep, back_low)
EPSILON = 1e-05

def matmul(left, right):
    return jnp.dot(left, right, precision=lax.Precision.HIGHEST, preferred_element_type=jnp.float32)

def gelu(value):
    return 0.5 * value * (1.0 + jnp.tanh(0.7978845608028654 * (value + 0.044715 * value * value * value)))

def normalize(value, gain, shift):
    center = lax.optimization_barrier(jnp.mean(value, -1, keepdims=True))
    spread = lax.optimization_barrier(jnp.mean(value * value, -1, keepdims=True)) - center * center
    return (value - center) * lax.rsqrt(spread + EPSILON) * gain + shift

def layer(params, inputs):
    gain_one, shift_one, weight_qkv, bias_pair, weight_out, bias_out, gain_two, shift_two, weight_up, bias_up, weight_down, bias_down = params
    normed_one = low(normalize(inputs, gain_one, shift_one))
    pair = bias_pair.reshape(HEADS, 2, HEAD)
    full_bias = jnp.stack([pair[:, 0], jnp.zeros_like(pair[:, 0]), pair[:, 1]], 1).reshape(3 * D)
    joined = low_back(low(matmul(normed_one, weight_qkv) + full_bias)).reshape(LEN, HEADS, 3, HEAD)
    query = joined[:, :, 0]
    keys = joined[:, :, 1]
    values = joined[:, :, 2]
    raw = jnp.einsum('qhe,khe->hqk', query, keys, precision=lax.Precision.HIGHEST) * 0.125
    place = jnp.arange(LEN)
    distance = (place[:, None] - place[None, :]).astype(jnp.float32)
    slopes = 2.0 ** (-8.0 * (jnp.arange(HEADS).astype(jnp.float32) + 1.0) / HEADS)
    scores = raw - slopes[:, None, None] * distance[None]
    scores = low_back(jnp.where(distance[None] >= 0, scores, -jnp.inf))
    top = lax.optimization_barrier(jnp.max(scores, -1, keepdims=True))
    expo = jnp.exp(scores - top)
    probs = low(expo / lax.optimization_barrier(jnp.sum(expo, -1, keepdims=True)))
    context = jnp.einsum('hqk,khe->qhe', probs, values, precision=lax.Precision.HIGHEST).reshape(LEN, D)
    context = low_back(low(context))
    middle = inputs + low_back(matmul(context, weight_out)) + bias_out
    normed_two = low(normalize(middle, gain_two, shift_two))
    hidden = low_back(matmul(normed_two, weight_up) + bias_up)
    active = low(gelu(hidden))
    return middle + low_back(matmul(active, weight_down)) + bias_down

def reference(x_in, ln1_gain, ln1_bias, w_qkv, bias_qv, w_out, b_out, ln2_gain, ln2_bias, w_up, b_up, w_down, b_down, grad_out):
    params = tuple((item.astype(jnp.float32) for item in (ln1_gain, ln1_bias, w_qkv, bias_qv, w_out, b_out, ln2_gain, ln2_bias, w_up, b_up, w_down, b_down)))
    inputs = x_in.astype(jnp.float32).reshape(-1, LEN, D)
    cotangent = grad_out.astype(jnp.float32).reshape(-1, LEN, D)

    def advance(total, pair):
        value, pull = jax.vjp(layer, params, pair[0])
        grad_params, grad_inputs = pull(pair[1])
        total = jax.tree.map(lambda first, second: first + second, total, grad_params)
        return (total, (value.astype(jnp.bfloat16), grad_inputs.astype(jnp.bfloat16)))
    start = jax.tree.map(jnp.zeros_like, params)
    total, (outputs, grad_inputs) = lax.scan(advance, start, (inputs, cotangent))
    return (outputs.reshape(-1, D), grad_inputs.reshape(-1, D), total[0], total[1], total[2], total[3], total[4], total[5], total[6], total[7], total[8], total[9], total[10], total[11])
```

```python
import functools

import jax
import jax.numpy as jnp
from jax import lax
from jax.experimental import pallas as pl
from jax.experimental.pallas import tpu as pltpu
from jax.sharding import Mesh, PartitionSpec as P

D = 1024
HEADS = 16
HEAD = 64
LEN = 1024
EPSILON = 1e-05
BLOCK = 256
LOW = jnp.bfloat16
F32 = jnp.float32
SWAP = [(0, 1), (1, 0)]


def dot(left, right, left_axis, right_axis):
    return lax.dot_general(
        left, right, (((left_axis,), (right_axis,)), ((), ())), preferred_element_type=F32
    )


def swap(value):
    return lax.ppermute(value, "core", SWAP)


def half_of(value, which):
    rows = value.shape[0] // 2
    return lax.dynamic_slice_in_dim(value, which * rows, rows, 0)


def join_cores(value):
    first = lax.axis_index("core") == 0
    other = swap(value)
    return jnp.concatenate(
        [jnp.where(first, value, other), jnp.where(first, other, value)], 0
    )


def sum_cores(partial):
    core = lax.axis_index("core")
    return half_of(partial, core) + swap(half_of(partial, 1 - core))


def tokens_in(value):
    rows, width = value.shape
    core = lax.axis_index("core")
    halves = value.reshape(rows // LEN, 2, LEN // 2, width)
    mine = lax.dynamic_index_in_dim(halves, core, 1, False)
    other = swap(lax.dynamic_index_in_dim(halves, 1 - core, 1, False))
    both = jnp.concatenate(
        [jnp.where(core == 0, mine, other), jnp.where(core == 0, other, mine)], 0
    ).reshape(rows, width)
    return lax.all_to_all(both, "row", 0, 1, tiled=True)


def tokens_out(value):
    core = lax.axis_index("core")
    both = lax.all_to_all(value, "row", 1, 0, tiled=True)
    rows, width = both.shape
    parts = both.reshape(2, rows // LEN, LEN // 2, width)
    mine = lax.dynamic_index_in_dim(parts, core, 0, False)
    other = swap(lax.dynamic_index_in_dim(parts, 1 - core, 0, False))
    return jnp.stack(
        [jnp.where(core == 0, mine, other), jnp.where(core == 0, other, mine)], 1
    ).reshape(rows, width)


def ring(axis, step):
    count = lax.axis_size(axis)
    return [(i, (i + step) % count) for i in range(count)]


def gather_axis(value, axis):
    count, me = lax.axis_size(axis), lax.axis_index(axis)
    held = [value] + [lax.ppermute(value, axis, ring(axis, -k)) for k in range(1, count)]
    if count == 2:
        return jnp.where(me == 0, jnp.stack(held), jnp.stack(held[::-1]))
    return jnp.take(jnp.stack(held), (jnp.arange(count) - me) % count, axis=0)


def scatter_axis(value, axis):
    count, me = lax.axis_size(axis), lax.axis_index(axis)
    total = lax.dynamic_index_in_dim(value, me, 0, False).astype(F32)
    for k in range(1, count):
        block = lax.dynamic_index_in_dim(value, (me + k) % count, 0, False)
        total = total + lax.ppermute(block.astype(LOW), axis, ring(axis, k)).astype(F32)
    return total


def gather_weight(weight, row_first):
    rows, width = weight.shape
    size = lax.axis_size("dp")
    me = lax.axis_index("dp")
    piece = rows // 2 // size
    wanted = (["row", "y"] if row_first else ["y", "row"]) + ["dp", "rows", "width"]
    halves = []
    for half, axes in enumerate((("row", "y", "dp"), ("row", "dp", "y"))):
        part = lax.dynamic_slice_in_dim(weight, half * (rows // 2) + me * piece, piece, 0)
        for axis in axes:
            part = gather_axis(part, axis)
        names = list(axes[::-1]) + ["rows", "width"]
        part = part.transpose([names.index(name) for name in wanted])
        halves.append(part.reshape(part.shape[:2] + (rows // 2, width)))
    return jnp.concatenate(halves, 2)


def scatter_grad(grad, row_first):
    rows, width = grad.shape[2:]
    count = lax.axis_size("dp")
    names = (["row", "y"] if row_first else ["y", "row"]) + ["half", "dp", "rows", "width"]
    grad = grad.reshape(grad.shape[:2] + (2, count, rows // 2 // count, width))
    halves = []
    for half, axes in enumerate((("dp", "y", "row"), ("y", "dp", "row"))):
        order = ["half"] + list(axes) + ["rows", "width"]
        part = grad.transpose([names.index(name) for name in order])[half]
        for axis in axes:
            part = scatter_axis(part, axis)
        part = gather_axis(part.astype(LOW), "dp")
        halves.append(part.reshape(rows // 2, width))
    return jnp.concatenate(halves, 0).astype(F32)


def norm_forward(values, gain, shift):
    center = jnp.sum(values, 1, keepdims=True) / D
    spread = jnp.sum(values * values, 1, keepdims=True) / D - center * center
    inverse = lax.rsqrt(spread + EPSILON)
    scaled = (values - center) * inverse
    return (scaled * gain + shift).astype(LOW), scaled, inverse


def norm_backward(grad_normed, scaled, inverse, gain):
    product = grad_normed * gain
    first = jnp.sum(product, 1, keepdims=True) / D
    second = jnp.sum(product * scaled, 1, keepdims=True) / D
    grad_values = inverse * (product - first - scaled * second)
    return grad_values, jnp.sum(grad_normed * scaled, 0), jnp.sum(grad_normed, 0)


def scores_block(keys, query, slope, index):
    count = keys.shape[0]
    raw = dot(keys, query, 1, 1)
    key_place = lax.broadcasted_iota(jnp.int32, (count, 1), 0)
    query_place = lax.broadcasted_iota(jnp.int32, (1, BLOCK), 1) + index * BLOCK
    distance = query_place.astype(F32) - key_place.astype(F32)
    scores = raw - slope * distance
    edge = count - BLOCK
    seen = key_place[edge:] <= query_place
    last = jnp.where(seen, scores[edge:], -jnp.inf)
    return last if edge == 0 else jnp.concatenate([scores[:edge], last], 0)


def attend_kernel(slope_ref, joined_ref, context_ref, log_ref):
    step = pl.program_id(0)
    for index in range(LEN // BLOCK):
        end = (index + 1) * BLOCK
        rows = pl.ds(index * BLOCK, BLOCK)
        parts = []
        for head in range(2):
            base = head * 3 * HEAD
            query = joined_ref[0, rows, base : base + HEAD] * LOW(0.125)
            keys = joined_ref[0, :end, base + HEAD : base + 2 * HEAD]
            values = joined_ref[0, :end, base + 2 * HEAD : base + 3 * HEAD]
            scores = scores_block(keys, query, slope_ref[step * 2 + head], index)
            top = jnp.max(scores, 0, keepdims=True)
            expo = jnp.exp(scores - top)
            total = jnp.sum(expo, 0, keepdims=True)
            parts.append(dot(values, expo.astype(LOW), 0, 0) * (1.0 / total))
            log_ref[0, head : head + 1, rows] = top + jnp.log(total)
        context_ref[0, rows, :] = jnp.concatenate(parts, 0).T.astype(LOW)


def attend_back_kernel(slope_ref, joined_ref, grad_ref, log_ref, out_ref, keys_acc, values_acc):
    step = pl.program_id(0)
    for index in reversed(range(LEN // BLOCK)):
        end = (index + 1) * BLOCK
        rows = pl.ds(index * BLOCK, BLOCK)
        for head in range(2):
            base = head * 3 * HEAD
            query = joined_ref[0, rows, base : base + HEAD] * LOW(0.125)
            keys = joined_ref[0, :end, base + HEAD : base + 2 * HEAD]
            values = joined_ref[0, :end, base + 2 * HEAD : base + 3 * HEAD]
            grad = grad_ref[0, rows, head * HEAD : (head + 1) * HEAD]
            scores = scores_block(keys, query, slope_ref[step * 2 + head], index)
            probs = jnp.exp(scores - log_ref[0, head : head + 1, rows])
            grad_probs = dot(values, grad, 1, 1)
            weighted = probs * grad_probs
            inner = jnp.sum(weighted, 0, keepdims=True)
            grad_scores = (weighted - probs * inner).astype(LOW)
            grad_query = dot(keys, grad_scores, 0, 0) * 0.125
            out_ref[0, rows, base : base + HEAD] = grad_query.T.astype(LOW)
            grad_keys = dot(grad_scores, query, 1, 0)
            grad_values = dot(probs.astype(LOW), grad, 1, 0)
            if end == LEN:
                keys_acc[head] = grad_keys
                values_acc[head] = grad_values
            else:
                keys_acc[head, :end] += grad_keys
                values_acc[head, :end] += grad_values
    for head in range(2):
        base = head * 3 * HEAD
        out_ref[0, :, base + HEAD : base + 2 * HEAD] = keys_acc[head].astype(LOW)
        out_ref[0, :, base + 2 * HEAD : base + 3 * HEAD] = values_acc[head].astype(LOW)


VMEM_LIMIT = 48 * 1024 * 1024


def pair_spec(width, pairs, count):
    return pl.BlockSpec(
        (1, LEN, width),
        lambda step, seq: (step // pairs, seq, step % pairs),
    )


def attend(joined, slopes):
    blocks, tokens, width = joined.shape
    pairs = width // (6 * HEAD)
    count = tokens // LEN
    return pl.pallas_call(
        attend_kernel,
        grid=(blocks * pairs, count),
        in_specs=[
            pl.BlockSpec(memory_space=pltpu.SMEM),
            pair_spec(6 * HEAD, pairs, count),
        ],
        out_specs=[
            pair_spec(2 * HEAD, pairs, count),
            pl.BlockSpec((1, 2, LEN), lambda step, seq: (step, 0, seq)),
        ],
        out_shape=[
            jax.ShapeDtypeStruct((blocks, tokens, width // 3), LOW),
            jax.ShapeDtypeStruct((blocks * pairs, 2, tokens), F32),
        ],
        compiler_params=pltpu.CompilerParams(vmem_limit_bytes=VMEM_LIMIT),
        cost_estimate=pl.CostEstimate(
            flops=40_000_000_000, bytes_accessed=8_000_000, transcendentals=0
        ),
        name="attend",
    )(slopes, joined)


def attend_back(joined, grad_context, logs, slopes):
    blocks, tokens, width = joined.shape
    pairs = width // (6 * HEAD)
    count = tokens // LEN
    return pl.pallas_call(
        attend_back_kernel,
        grid=(blocks * pairs, count),
        in_specs=[
            pl.BlockSpec(memory_space=pltpu.SMEM),
            pair_spec(6 * HEAD, pairs, count),
            pair_spec(2 * HEAD, pairs, count),
            pl.BlockSpec((1, 2, LEN), lambda step, seq: (step, 0, seq)),
        ],
        out_specs=pair_spec(6 * HEAD, pairs, count),
        out_shape=jax.ShapeDtypeStruct(joined.shape, LOW),
        scratch_shapes=[pltpu.VMEM((2, LEN, HEAD), F32), pltpu.VMEM((2, LEN, HEAD), F32)],
        compiler_params=pltpu.CompilerParams(vmem_limit_bytes=VMEM_LIMIT),
        cost_estimate=pl.CostEstimate(
            flops=80_000_000_000, bytes_accessed=12_000_000, transcendentals=0
        ),
        name="attend_back",
    )(slopes, joined, grad_context, logs)


def on_device(
    x_in,
    ln1_gain,
    ln1_bias,
    w_qkv,
    bias_qv,
    w_out,
    b_out,
    ln2_gain,
    ln2_bias,
    w_up,
    b_up,
    w_down,
    b_down,
    grad_out,
):
    row = lax.axis_index("row")
    column = lax.axis_index("y")
    core = lax.axis_index("core")
    row_count = lax.axis_size("row")
    blocks = lax.axis_size("y")
    part = x_in.shape[1]
    local_heads = w_qkv.shape[1] // (3 * HEAD)
    hidden_width = w_up.shape[1]
    out_rows = w_out.shape[0]

    block_ids = jnp.arange(blocks) * 2 + core
    head_ids = (block_ids[:, None] * local_heads + jnp.arange(local_heads)).reshape(-1)
    slopes = 2.0 ** (-8.0 * (head_ids.astype(F32) + 1.0) / HEADS)

    inputs = tokens_in(x_in).astype(F32)
    small = jnp.concatenate(
        [ln1_gain, ln1_bias, b_out, ln2_gain, ln2_bias, b_down, bias_qv, b_up]
    )
    small_all = lax.all_gather(small, ("row", "y"), axis=0).reshape(row_count, blocks, -1)
    by_feature = small_all[:, 0, : 6 * part].reshape(row_count, 6, part)
    by_feature = by_feature.transpose(1, 0, 2).reshape(6, D)
    gain_one, shift_one, bias_out, gain_two, shift_two, bias_down = by_feature
    pair = small_all[0, :, 6 * part : 6 * part + bias_qv.shape[0]]
    pair = pair.reshape(blocks, local_heads, 2, HEAD)
    full_bias = jnp.stack(
        [pair[:, :, 0], jnp.zeros_like(pair[:, :, 0]), pair[:, :, 1]], 2
    ).reshape(blocks, 1, -1)
    bias_up = small_all[0, :, 6 * part + bias_qv.shape[0] :].reshape(blocks, 1, -1)

    qkv_all = gather_weight(w_qkv, False).reshape(blocks, D, -1)
    out_all = gather_weight(w_out, True)
    out_all = out_all.transpose(1, 2, 0, 3).reshape(blocks, out_rows, D)
    up_all = gather_weight(w_up, False).reshape(blocks, D, -1)
    down_all = gather_weight(w_down, True)
    down_all = down_all.transpose(1, 2, 0, 3).reshape(blocks, hidden_width, D)

    normed_one, scaled_one, inverse_one = norm_forward(inputs, gain_one, shift_one)
    normed_one = join_cores(normed_one)
    joined = jnp.stack(
        [
            (dot(normed_one, qkv_all[i], 1, 0) + full_bias[i]).astype(LOW)
            for i in range(blocks)
        ]
    )
    context, logs = attend(joined, slopes)
    mixed = sum(dot(context[i], out_all[i], 1, 0) for i in range(blocks))
    middle = inputs + sum_cores(mixed) + bias_out
    normed_two, scaled_two, inverse_two = norm_forward(middle, gain_two, shift_two)
    normed_two = join_cores(normed_two)
    active, slope_of = [], []
    for i in range(blocks):
        hidden = dot(normed_two, up_all[i], 1, 0) + bias_up[i]
        bent = jnp.tanh(0.7978845608028654 * (hidden + 0.044715 * hidden * hidden * hidden))
        active.append((0.5 * hidden * (1.0 + bent)).astype(LOW))
        slope_of.append(
            0.5 * (1.0 + bent)
            + 0.5
            * hidden
            * (1.0 - bent * bent)
            * 0.7978845608028654
            * (1.0 + 3.0 * 0.044715 * hidden * hidden)
        )
    lifted = sum(dot(active[i], down_all[i], 1, 0) for i in range(blocks))
    out = (middle + sum_cores(lifted) + bias_down).astype(LOW)
    out = tokens_out(out)

    grad_low = tokens_in(grad_out)
    cotangent = grad_low.astype(F32)
    grad_b_down = jnp.sum(cotangent, 0)
    grad_all = join_cores(grad_low)

    def split_columns(parts):
        whole = jnp.stack([item.astype(LOW) for item in parts])
        return whole.reshape(blocks, -1, row_count, part).transpose(2, 0, 1, 3)

    def split_rows(parts):
        whole = jnp.stack([item.astype(LOW) for item in parts])
        return whole.reshape(blocks, row_count, part, -1)

    grad_down = scatter_grad(
        split_columns([dot(active[i], grad_all, 0, 0) for i in range(blocks)]), True
    )
    grad_hidden = [
        (dot(grad_all, down_all[i], 1, 1) * slope_of[i]).astype(LOW) for i in range(blocks)
    ]
    grad_b_up = jnp.stack([jnp.sum(item.astype(F32), 0) for item in grad_hidden])
    grad_up = scatter_grad(
        split_rows([dot(normed_two, item, 0, 0) for item in grad_hidden]), False
    )
    grad_normed_two = sum_cores(sum(dot(grad_hidden[i], up_all[i], 1, 1) for i in range(blocks)))
    back_two, grad_ln2_gain, grad_ln2_bias = norm_backward(
        grad_normed_two, scaled_two, inverse_two, gain_two
    )
    grad_middle = cotangent + back_two
    grad_b_out = jnp.sum(grad_middle, 0)
    grad_middle_all = join_cores(grad_middle.astype(LOW))
    grad_w_out = scatter_grad(
        split_columns([dot(context[i], grad_middle_all, 0, 0) for i in range(blocks)]),
        True,
    )
    grad_context = jnp.stack(
        [dot(grad_middle_all, out_all[i], 1, 1).astype(LOW) for i in range(blocks)]
    )
    grad_joined = attend_back(joined, grad_context, logs, slopes)
    totals = jnp.sum(grad_joined.astype(F32), 1).reshape(blocks, local_heads, 3, HEAD)
    grad_bias_qv = jnp.stack([totals[:, :, 0], totals[:, :, 2]], 2).reshape(blocks, -1)
    grad_qkv = scatter_grad(
        split_rows([dot(normed_one, grad_joined[i], 0, 0) for i in range(blocks)]),
        False,
    )
    grad_normed_one = sum_cores(sum(dot(grad_joined[i], qkv_all[i], 1, 1) for i in range(blocks)))
    back_one, grad_ln1_gain, grad_ln1_bias = norm_backward(
        grad_normed_one, scaled_one, inverse_one, gain_one
    )
    grad_input = tokens_out((grad_middle + back_one).astype(LOW))

    features = jnp.stack(
        [grad_ln1_gain, grad_ln1_bias, grad_b_out, grad_ln2_gain, grad_ln2_bias, grad_b_down]
    )
    columns = jnp.concatenate([grad_bias_qv, grad_b_up], 1)
    features = features + swap(features)
    sums = lax.psum(
        jnp.concatenate([features.reshape(-1), columns.reshape(-1)]), ("dp", "row", "y")
    )
    features = sums[: 6 * D].reshape(6, D)
    features = lax.dynamic_slice_in_dim(features, row * part, part, 1)
    columns = sums[6 * D :].reshape(blocks, -1)
    columns = lax.dynamic_index_in_dim(columns, column, 0, False)
    cut = bias_qv.shape[0]
    return (
        out,
        grad_input,
        features[0],
        features[1],
        grad_qkv,
        columns[:cut],
        grad_w_out,
        features[2],
        features[3],
        features[4],
        grad_up,
        columns[cut:],
        grad_down,
        features[5],
    )


def solution(mesh):
    dp, rows, cols = (mesh.shape[name] for name in ("dp", "row", "col"))
    split = Mesh(mesh.devices.reshape(dp, rows, cols // 2, 2), ("dp", "row", "y", "core"))
    col = ("y", "core")
    token = P(("dp",) + col, "row")
    feature = P("row")
    column = P(col)
    wide = P("row", col)
    tall = P(col, "row")
    in_specs = (
        token,
        feature,
        feature,
        wide,
        column,
        tall,
        feature,
        feature,
        feature,
        wide,
        column,
        tall,
        feature,
        token,
    )
    out_specs = (
        token,
        token,
        feature,
        feature,
        wide,
        column,
        tall,
        feature,
        feature,
        feature,
        wide,
        column,
        tall,
        feature,
    )
    return jax.shard_map(
        on_device, mesh=split, in_specs=in_specs, out_specs=out_specs, check_vma=False
    )
```
